32 devices in a mesh: context: 4 (over z), head: 4 (over y, x), dp: 2 (over core).
Axes of the slice: x: 2, y: 2, z: 4, core: 2. Of those that a mesh axis runs over, the one named last changes fastest.
Arguments:
- query_tok: bfloat16 [2, 2, 512, 5120], P('dp', None, ('context', 'head')), may hold values from -6 to 6
- key_tok: bfloat16 [2, 2, 512, 5120], P('dp', None, ('context', 'head')), may hold values from -6 to 6
- value_tok: bfloat16 [2, 2, 512, 5120], P('dp', None, ('context', 'head')), may hold values from -6 to 6
- token_rates: bfloat16 [2, 2, 512, 40], P('dp', None, ('context', 'head')), may hold values from 0.02 to 3, as said below
- fast_init: bfloat16 [3, 40, 128, 256], P(None, 'head', 'dp'), may hold values from -0.5 to 0.5
- out_gain: bfloat16 [5120], P('head'), may hold values from 0.5 to 1.5
Outputs:
- head_out: bfloat16 [2, 2, 512, 5120], P('dp', None, 'context', 'head')
- fast_final: float32 [2, 3, 40, 128, 256], P('dp', None, 'head')
The draws below stay inside these ranges and needn't reach their ends.
Inputs may be any that keep to these rules, and one draw needn't show every extreme that they name: `token_rates`: positive learning rates of each token and head.
All inputs are finite; a program needn't handle non-finite values.
Results may differ from the reference program's by a relative error of at most 0.0064.
Values may be sent and summed in bfloat16 or wider, within the bound.
A program may use at most 128 MiB of HBM per device.

```python
import jax
import jax.numpy as jnp
from jax import lax

HEADS = 40
DH = 128
HF = 256
BLOCKS = 2
NS_STEPS = 5
D = 5120
GROUP = 512
SAMPLES = 2


def draw_token_rates(key, part):
    key = jax.random.fold_in(key, 11)
    position = jnp.arange(GROUP, dtype=jnp.float32)[None, None, :, None] / GROUP
    shape_all = (SAMPLES, BLOCKS, GROUP, HEADS)
    jitter = jax.random.uniform(key, shape_all, jnp.float32, -1.0, 1.0)
    drawn = 0.15 * jnp.exp(jitter) * (1.0 + 2.5 * position)
    return drawn.astype(jnp.bfloat16)


def level_of(key, extent, pieces, smallest, top_value):
    def one(dim, blocks):
        draws = jax.random.uniform(jax.random.fold_in(jax.random.fold_in(key, 6), dim), (blocks,), jnp.float32, smallest / len(pieces), top_value / len(pieces))
        return jnp.repeat(jnp.exp(draws), extent[dim] // blocks).reshape((-1,) + (1,) * (len(extent) - dim - 1))

    factor_of = one(*pieces[0])
    for cut in pieces[1:]:
        factor_of = factor_of * one(*cut)
    return factor_of


def noise(stream_key, dims, spread, bound, cuts=(), kind=jnp.bfloat16):
    entries = jax.random.normal(stream_key, dims, jnp.float32) * spread
    if len(cuts) > 0:
        entries = level_of(stream_key, dims, cuts, -0.22, 0.18) * entries
    return jnp.clip(entries, min=-bound, max=bound).astype(kind)


def setup_inputs(seed: int = 0) -> dict:
    key_list = jax.random.split(jax.random.key(seed), 7)
    query_tok = noise(key_list[0], (SAMPLES, BLOCKS, GROUP, D), 1.0, 6.0, ((0, 2), (2, 16)))
    key_tok = noise(key_list[1], (SAMPLES, BLOCKS, GROUP, D), 1.0, 6.0, ((0, 2), (2, 16)))
    value_tok = noise(key_list[2], (SAMPLES, BLOCKS, GROUP, D), 1.0, 6.0, ((0, 2), (2, 16)))
    token_rates = draw_token_rates(jax.random.fold_in(key_list[6], 71), 0)
    fast_init = noise(key_list[4], (3, HEADS, DH, HF), DH ** -0.5, 0.5, ((1, 4), (2, 2)))
    out_gain = jnp.clip(1.0 + 0.1 * jax.random.normal(key_list[5], (D,), jnp.float32), 0.5, 1.5).astype(jnp.bfloat16)
    return dict(query_tok=query_tok, key_tok=key_tok, value_tok=value_tok, token_rates=token_rates, fast_init=fast_init, out_gain=out_gain)


schulz_coeffs = (3.4445, -4.775, 2.0315)

def orthogonalize(grads):
    frob = jnp.sqrt(lax.optimization_barrier(jnp.sum(grads * grads, axis=(1, 2), keepdims=True))) + 1e-07
    ortho = grads / frob
    for sweep in range(NS_STEPS):
        gram = jnp.einsum('nij,nkj->nik', ortho, ortho, precision=lax.Precision.HIGHEST)
        poly = schulz_coeffs[1] * gram + schulz_coeffs[2] * jnp.einsum('nij,njk->nik', gram, gram, precision=lax.Precision.HIGHEST)
        ortho = schulz_coeffs[0] * ortho + jnp.einsum('nij,njk->nik', poly, ortho, precision=lax.Precision.HIGHEST)
    return ortho

def head_layer(query_h, key_h, value_h, rate_h, init_h, gain_h):
    fast_state = init_h.astype(jnp.float32)
    init_norm = jnp.sqrt(lax.optimization_barrier(jnp.sum(fast_state * fast_state, axis=1, keepdims=True)))
    gain_f = gain_h.astype(jnp.float32)
    results = []
    for block_idx in range(BLOCKS):
        weights = fast_state.astype(jnp.bfloat16)
        queries = query_h[block_idx]
        keys_blk = key_h[block_idx]
        vals = value_h[block_idx]
        pre_gate = jnp.dot(queries, weights[0], preferred_element_type=jnp.float32)
        pre_up = jnp.dot(queries, weights[1], preferred_element_type=jnp.float32)
        hidden_q = (jax.nn.silu(pre_gate) * pre_up).astype(jnp.bfloat16)
        mapped = jnp.dot(hidden_q, weights[2].T, preferred_element_type=jnp.float32)
        mean_sq = lax.optimization_barrier(jnp.mean(mapped * mapped, axis=-1, keepdims=True))
        results.append((mapped * lax.rsqrt(mean_sq + 1e-06) * gain_f).astype(jnp.bfloat16))
        key_gate = jnp.dot(keys_blk, weights[0], preferred_element_type=jnp.float32)
        key_up = jnp.dot(keys_blk, weights[1], preferred_element_type=jnp.float32)
        sigma = jax.nn.sigmoid(key_gate)
        act_gate = key_gate * sigma
        slope = sigma * (1.0 + key_gate * (1.0 - sigma))
        hidden_k = (act_gate * key_up).astype(jnp.bfloat16)
        rate_col = rate_h[block_idx].astype(jnp.float32)[:, None]
        back = jnp.dot(vals, weights[2], preferred_element_type=jnp.float32)
        grad_up_in = (rate_col * back * act_gate).astype(jnp.bfloat16)
        grad_gate_in = (rate_col * back * key_up * slope).astype(jnp.bfloat16)
        rated_value = (rate_col * vals.astype(jnp.float32)).astype(jnp.bfloat16)
        grads = jnp.stack([jnp.dot(keys_blk.T, grad_gate_in, preferred_element_type=jnp.float32), jnp.dot(keys_blk.T, grad_up_in, preferred_element_type=jnp.float32), jnp.dot(rated_value.T, hidden_k, preferred_element_type=jnp.float32)])
        step_size = jnp.sum(rate_col) / GROUP
        fast_state = fast_state + step_size * orthogonalize(grads)
        col_norm = jnp.sqrt(lax.optimization_barrier(jnp.sum(fast_state * fast_state, axis=1, keepdims=True)) + 1e-06)
        fast_state = fast_state * (init_norm / col_norm)
    return (jnp.stack(results), fast_state)

def reference(query_tok, key_tok, value_tok, token_rates, fast_init, out_gain):
    outputs = []
    finals = []
    init_heads = fast_init.transpose(1, 0, 2, 3)
    gain_heads = out_gain.reshape(HEADS, DH)
    for sample in range(SAMPLES):
        query_heads = query_tok[sample].reshape(BLOCKS, GROUP, HEADS, DH).transpose(2, 0, 1, 3)
        key_heads = key_tok[sample].reshape(BLOCKS, GROUP, HEADS, DH).transpose(2, 0, 1, 3)
        value_heads = value_tok[sample].reshape(BLOCKS, GROUP, HEADS, DH).transpose(2, 0, 1, 3)
        rate_heads = token_rates[sample].transpose(2, 0, 1)

        def one_head(packed):
            return head_layer(*packed)
        head_res, head_fin = lax.map(one_head, (query_heads, key_heads, value_heads, rate_heads, init_heads, gain_heads))
        outputs.append(head_res.transpose(1, 2, 0, 3).reshape(BLOCKS, GROUP, HEADS * DH))
        finals.append(head_fin.transpose(1, 0, 2, 3))
    return (jnp.stack(outputs), jnp.stack(finals))
```

```python
import functools

import jax
import jax.numpy as jnp
from jax import lax
from jax.experimental import pallas as pl
from jax.experimental.pallas import tpu as pltpu
from jax.sharding import PartitionSpec as P

NS_STEPS = 5
COEFFS = (3.4445, -4.775, 2.0315)
MESH = pl.DeviceIdType.MESH
F32 = jnp.float32
BF16 = jnp.bfloat16


def dot(a, b, ca=1, cb=0):
    return lax.dot_general(a, b, (((ca,), (cb,)), ((), ())), preferred_element_type=F32)


def split(x):
    high = x.astype(BF16)
    return high, (x - high.astype(F32)).astype(BF16)


def schulz_step(ortho):
    xh, xl = split(ortho)
    both = dot(xh, jnp.concatenate([xh, xl], axis=0), 1, 1)
    half = both.shape[1] // 2
    cross = both[:, half:]
    gram = both[:, :half] + cross + cross.T
    gh, gl = split(gram)
    both = dot(gh, jnp.concatenate([gh, gl], axis=1))
    cross = both[:, half:]
    poly = COEFFS[1] * gram + COEFFS[2] * (both[:, :half] + cross + cross.T)
    ph, pl_ = split(poly)
    moved = dot(jnp.concatenate([ph, pl_], axis=1), jnp.concatenate([xh, xh], axis=0)) + dot(ph, xl)
    return COEFFS[0] * ortho + moved


def kernel(
    dims,
    q_ref, k_ref, v_ref, r_ref, w_ref, gain_ref,
    out_ref, fin_ref,
    q_buf, k_buf, v_buf, r_buf, w_buf, o_stage, f_stage,
    w_now, w_bf, g_acc,
    tok_send, tok_recv, r_send, r_recv, w_send, w_recv, out_send, out_recv, fin_send, fin_recv,
):
    contexts, groups, heads, blocks, rows, dh, hf = dims
    peers = contexts * groups
    tokens = peers * rows
    local_tokens = groups * rows
    ctx, grp, core = lax.axis_index("context"), lax.axis_index("head"), lax.axis_index("dp")
    me = ctx * groups + grp

    def first_head(c):
        return (c * heads) // contexts

    own_first = first_head(ctx)
    own_count = first_head(ctx + 1) - own_first
    most = -(-heads // contexts)

    barrier = pltpu.get_barrier_semaphore()

    def greet(i, carry):
        peer = (me + i) % peers
        pl.semaphore_signal(barrier, inc=1, device_id=(peer // groups, peer % groups, core), device_id_type=MESH)
        return carry

    lax.fori_loop(1, peers, greet, 0)
    pl.semaphore_signal(barrier, inc=1, device_id=(ctx, grp, 1 - core), device_id_type=MESH)
    pl.semaphore_wait(barrier, peers)

    my_rows = pl.ds(pl.multiple_of(core * (dh // 2), dh // 2), dh // 2)
    w_src = w_ref.at[:, pl.ds(jnp.minimum(own_first, heads - most), most)]
    w_dst = w_buf.at[:, :, my_rows, :]
    w_remote = pltpu.make_async_remote_copy(
        w_src, w_dst, w_send, w_recv, device_id=(ctx, grp, 1 - core), device_id_type=MESH
    )
    w_remote.start()
    pltpu.make_async_copy(w_src, w_dst, w_recv).start()

    my_tokens = pl.ds(pl.multiple_of(me * rows, rows), rows)
    r_dst = r_buf.at[:, my_tokens, :]
    pltpu.make_async_copy(r_ref.at[0], r_dst, r_recv).start()

    def send_rates(i, carry):
        peer = (me + i) % peers
        pltpu.make_async_remote_copy(
            r_ref.at[0], r_dst, r_send, r_recv,
            device_id=(peer // groups, peer % groups, core), device_id_type=MESH,
        ).start()
        return carry

    lax.fori_loop(1, peers, send_rates, 0)

    arrays = ((k_ref, k_buf), (v_ref, v_buf), (q_ref, q_buf))

    def columns_of(c, g, j):
        return pl.ds(pl.multiple_of((g * heads + first_head(c) + j) * dh, dh), dh)

    def send_head(j, carry):
        for which in ((0, 1), (2,)):
            @pl.when(j < own_count)
            def _():
                for a in which:
                    src, buf = arrays[a]
                    pltpu.make_async_copy(
                        src.at[0, :, :, columns_of(ctx, grp, j)], buf.at[j, :, my_tokens, :], tok_recv.at[a, j]
                    ).start()

            def send_to(i, inner):
                peer = (me + i) % peers
                c, g = peer // groups, peer % groups

                @pl.when(j < first_head(c + 1) - first_head(c))
                def _():
                    for a in which:
                        src, buf = arrays[a]
                        pltpu.make_async_remote_copy(
                            src.at[0, :, :, columns_of(c, g, j)], buf.at[j, :, my_tokens, :],
                            tok_send.at[a], tok_recv.at[a, j],
                            device_id=(c, g, core), device_id_type=MESH,
                        ).start()

                return inner

            lax.fori_loop(1, peers, send_to, 0)
        return carry

    lax.fori_loop(0, most, send_head, 0)

    def wait_for(ref, sem):
        pltpu.make_async_copy(ref, ref, sem).wait()

    wait_for(w_buf, w_recv)
    wait_for(r_buf, r_recv)

    chunk = min(tokens, 512)
    chunks = tokens // chunk

    def work(j, carry):
        shift = own_first - jnp.minimum(own_first, heads - most)
        lane = grp * heads + own_first + j
        init_sq = []
        for m in range(3):
            start = w_buf[m, shift + j].astype(F32)
            w_now[m] = start
            init_sq.append(jnp.sqrt(jnp.sum(start * start, axis=0, keepdims=True)))
        wait_for(k_buf.at[j], tok_recv.at[0, j])
        wait_for(v_buf.at[j], tok_recv.at[1, j])

        def block(b, norms):
            for m in range(3):
                w_bf[b, m] = w_now[m].astype(BF16)
                g_acc[m] = jnp.zeros((dh, hf), F32)

            def part(i, total):
                at = pl.ds(pl.multiple_of(i * chunk, chunk), chunk)
                keys, vals = k_buf[j, b, at, :], v_buf[j, b, at, :]
                rate_all = r_buf[b, at, :].astype(F32)
                lanes = lax.broadcasted_iota(jnp.int32, rate_all.shape, 1)
                rate = jnp.sum(jnp.where(lanes == lane, rate_all, 0.0), axis=1, keepdims=True)
                gate = dot(keys, w_bf[b, 0])
                up = dot(keys, w_bf[b, 1])
                back = dot(vals, w_bf[b, 2]) * rate
                sigma = jax.nn.sigmoid(gate)
                act = gate * sigma
                hidden = (act * up).astype(BF16)
                d_up = (back * act).astype(BF16)
                d_gate = (back * up * (sigma * (1.0 + gate * (1.0 - sigma)))).astype(BF16)
                rated = (vals.astype(F32) * rate).astype(BF16)
                g_acc[0] += dot(keys, d_gate, 0, 0)
                g_acc[1] += dot(keys, d_up, 0, 0)
                g_acc[2] += dot(rated, hidden, 0, 0)
                return total + jnp.sum(rate, axis=0, keepdims=True)

            eta = lax.fori_loop(0, chunks, part, jnp.zeros((1, 1), F32)) / tokens
            ortho = []
            for m in range(3):
                grad = g_acc[m]
                frob = jnp.sqrt(jnp.sum(jnp.sum(grad * grad, axis=0, keepdims=True), axis=1, keepdims=True)) + 1e-07
                ortho.append(grad / frob)
            ortho = lax.fori_loop(0, NS_STEPS, lambda s, xs: tuple(schulz_step(x) for x in xs), tuple(ortho))
            for m in range(3):
                moved = w_now[m] + eta * ortho[m]
                scale = norms[m] * lax.rsqrt(jnp.sum(moved * moved, axis=0, keepdims=True) + 1e-06)
                w_now[m] = moved * scale
            return norms

        lax.fori_loop(0, blocks, block, tuple(init_sq))

        for m in range(3):
            f_stage[j, m] = w_now[m].astype(BF16)
        head = own_first + j
        fin_dst = fin_ref.at[:, head]
        pltpu.make_async_copy(f_stage.at[j], fin_dst, fin_recv).start()

        def send_final(i, inner):
            pltpu.make_async_remote_copy(
                f_stage.at[j], fin_dst, fin_send.at[j, i], fin_recv,
                device_id=((ctx + i) % contexts, grp, core), device_id_type=MESH,
            ).start()
            return inner

        lax.fori_loop(1, contexts, send_final, 0)

        wait_for(q_buf.at[j], tok_recv.at[2, j])
        gain = gain_ref[head]

        def answer(b, inner):
            def part(i, innermost):
                at = pl.ds(pl.multiple_of(i * chunk, chunk), chunk)
                queries = q_buf[j, b, at, :]
                gate = dot(queries, w_bf[b, 0])
                up = dot(queries, w_bf[b, 1])
                hidden = (gate * jax.nn.sigmoid(gate) * up).astype(BF16)
                mapped = dot(hidden, w_bf[b, 2], 1, 1)
                mean_sq = jnp.mean(mapped * mapped, axis=1, keepdims=True)
                o_stage[j, b, at, :] = (mapped * lax.rsqrt(mean_sq + 1e-06) * gain).astype(BF16)
                return innermost

            lax.fori_loop(0, chunks, part, 0)
            return inner

        lax.fori_loop(0, blocks, answer, 0)

        out_dst = out_ref.at[0, :, :, pl.ds(pl.multiple_of(head * dh, dh), dh)]

        def of_context(c):
            return o_stage.at[j, :, pl.ds(pl.multiple_of(c * local_tokens, local_tokens), local_tokens), :]

        pltpu.make_async_copy(of_context(ctx), out_dst, out_recv).start()

        def send_out(i, inner):
            c = (ctx + i) % contexts
            pltpu.make_async_remote_copy(
                of_context(c), out_dst, out_send.at[j, i], out_recv,
                device_id=(c, grp, core), device_id_type=MESH,
            ).start()
            return inner

        lax.fori_loop(1, contexts, send_out, 0)
        return carry

    lax.fori_loop(0, own_count, work, 0)

    w_remote.wait_send()
    wait_for(r_buf.at[:, 0:tokens - rows, :], r_send)
    for count in sorted({heads // contexts, most}):
        @pl.when(own_count == count)
        def _():
            for a in range(3):
                src = arrays[a][0]
                wait_for(src.at[0, :, :, 0:(groups * heads - count) * dh], tok_send.at[a])

    def sent(j, carry):
        def one(i, inner):
            wait_for(f_stage.at[j], fin_send.at[j, i])
            wait_for(o_stage.at[j, :, 0:local_tokens, :], out_send.at[j, i])
            return inner

        return lax.fori_loop(1, contexts, one, carry)

    lax.fori_loop(0, own_count, sent, 0)
    wait_for(out_ref, out_recv)
    wait_for(fin_ref, fin_recv)


def body(contexts, groups, query_tok, key_tok, value_tok, token_rates, fast_init, out_gain):
    _, blocks, rows, _ = query_tok.shape
    _, heads, half, hf = fast_init.shape
    dh = 2 * half
    peers = contexts * groups
    tokens = peers * rows
    most = -(-heads // contexts)
    rates = jnp.pad(token_rates, ((0, 0), (0, 0), (0, 0), (0, 128 - token_rates.shape[3])))
    gain = out_gain.astype(F32).reshape(heads, 1, dh)
    dims = (contexts, groups, heads, blocks, rows, dh, hf)
    anywhere = pl.BlockSpec(memory_space=pl.ANY)
    tok = pltpu.VMEM((most, blocks, tokens, dh), BF16)
    dma = pltpu.SemaphoreType.DMA
    head_out, final = pl.pallas_call(
        functools.partial(kernel, dims),
        out_shape=(
            jax.ShapeDtypeStruct((1, blocks, groups * rows, heads * dh), BF16),
            jax.ShapeDtypeStruct((3, heads, dh, hf), BF16),
        ),
        in_specs=[anywhere] * 5 + [pl.BlockSpec(memory_space=pltpu.VMEM)],
        out_specs=(anywhere, anywhere),
        scratch_shapes=[
            tok, tok, tok,
            pltpu.VMEM((blocks, tokens, 128), BF16),
            pltpu.VMEM((3, most, dh, hf), BF16),
            tok,
            pltpu.VMEM((most, 3, dh, hf), BF16),
            pltpu.VMEM((3, dh, hf), F32),
            pltpu.VMEM((blocks, 3, dh, hf), BF16),
            pltpu.VMEM((3, dh, hf), F32),
            dma((3,)), dma((3, most)), dma, dma, dma, dma,
            dma((most, contexts)), dma, dma((most, contexts)), dma,
        ],
        compiler_params=pltpu.CompilerParams(
            collective_id=0, has_side_effects=True, vmem_limit_bytes=48 * 1024 * 1024
        ),
    )(query_tok, key_tok, value_tok, rates, fast_init, gain)
    return head_out, final.astype(F32)[None]


def solution(mesh):
    return jax.shard_map(
        functools.partial(body, mesh.shape["context"], mesh.shape["head"]),
        mesh=mesh,
        in_specs=(
            P("dp", None, ("context", "head"), None),
            P("dp", None, ("context", "head"), None),
            P("dp", None, ("context", "head"), None),
            P("dp", None, ("context", "head"), None),
            P(None, "head", "dp", None),
            P("head"),
        ),
        out_specs=(P("dp", None, "context", "head"), P("dp", None, "head", None, None)),
        check_vma=False,
    )
```

```python
import functools

import jax
import jax.numpy as jnp
from jax import lax
from jax.experimental import pallas as pl
from jax.experimental.pallas import tpu as pltpu
from jax.sharding import PartitionSpec as P

NS_STEPS = 5
COEFFS = (3.4445, -4.775, 2.0315)
MESH = pl.DeviceIdType.MESH
F32 = jnp.float32
BF16 = jnp.bfloat16


def dot(a, b, ca=1, cb=0):
    return lax.dot_general(a, b, (((ca,), (cb,)), ((), ())), preferred_element_type=F32)


def split(x):
    high = x.astype(BF16)
    return high, (x - high.astype(F32)).astype(BF16)


def schulz_step(ortho):
    xh, xl = split(ortho)
    both = dot(xh, jnp.concatenate([xh, xl], axis=0), 1, 1)
    half = both.shape[1] // 2
    cross = both[:, half:]
    gram = both[:, :half] + cross + cross.T
    gh, gl = split(gram)
    both = dot(gh, jnp.concatenate([gh, gl], axis=1))
    cross = both[:, half:]
    poly = COEFFS[1] * gram + COEFFS[2] * (both[:, :half] + cross + cross.T)
    ph, pl_ = split(poly)
    moved = dot(jnp.concatenate([ph, pl_], axis=1), jnp.concatenate([xh, xh], axis=0)) + dot(ph, xl)
    return COEFFS[0] * ortho + moved


def kernel(
    dims,
    q_ref, k_ref, v_ref, r_ref, w_ref, gain_ref,
    out_ref, fin_ref,
    q_buf, k_buf, v_buf, r_buf, w_buf, first_buf, first_out, o_stage, f_stage,
    w_now, w_bf, g_acc,
    tok_send, tok_recv, first_send, first_recv, r_send, r_recv, w_send, w_recv,
    out_send, out_recv, fin_send, fin_recv,
):
    contexts, groups, heads, blocks, rows, dh, hf = dims
    peers = contexts * groups
    tokens = peers * rows
    local_tokens = groups * rows
    ctx, grp, core = lax.axis_index("context"), lax.axis_index("head"), lax.axis_index("dp")
    me = ctx * groups + grp

    def first_head(c):
        return (c * heads) // contexts

    own_first = first_head(ctx)
    own_count = first_head(ctx + 1) - own_first
    most = -(-heads // contexts)

    barrier = pltpu.get_barrier_semaphore()

    def greet(i, carry):
        peer = (me + i) % peers
        pl.semaphore_signal(barrier, inc=1, device_id=(peer // groups, peer % groups, core), device_id_type=MESH)
        return carry

    lax.fori_loop(1, peers, greet, 0)
    pl.semaphore_signal(barrier, inc=1, device_id=(ctx, grp, 1 - core), device_id_type=MESH)
    pl.semaphore_wait(barrier, peers)

    my_rows = pl.ds(pl.multiple_of(core * (dh // 2), dh // 2), dh // 2)
    w_src = w_ref
    w_dst = w_buf.at[:, :, my_rows, :]
    w_remote = pltpu.make_async_remote_copy(
        w_src, w_dst, w_send, w_recv, device_id=(ctx, grp, 1 - core), device_id_type=MESH
    )
    w_remote.start()
    pltpu.make_async_copy(w_src, w_dst, w_recv).start()

    my_tokens = pl.ds(pl.multiple_of(me * rows, rows), rows)
    r_dst = r_buf.at[:, my_tokens, :]
    pltpu.make_async_copy(r_ref.at[0], r_dst, r_recv).start()

    def send_rates(i, carry):
        peer = (me + i) % peers
        pltpu.make_async_remote_copy(
            r_ref.at[0], r_dst, r_send, r_recv,
            device_id=(peer // groups, peer % groups, core), device_id_type=MESH,
        ).start()
        return carry

    lax.fori_loop(1, peers, send_rates, 0)

    later = blocks - 1
    arrays = ((k_ref, k_buf, blocks), (v_ref, v_buf, blocks), (q_ref, q_buf, later))

    def tokens_of(a, where):
        src, _, count = arrays[a]
        return src.at[0, pl.ds(blocks - count, count), :, where]

    def first_columns(g):
        return pl.ds(pl.multiple_of(g * heads * dh, heads * dh), heads * dh)

    first_dst = first_buf.at[pl.ds(pl.multiple_of(grp * rows, rows), rows), :]

    def send_first(i, carry):
        g = (grp + i) % groups
        pltpu.make_async_remote_copy(
            q_ref.at[0, 0, :, first_columns(g)], first_dst, first_send.at[i], first_recv,
            device_id=(ctx, g, core), device_id_type=MESH,
        ).start()
        return carry

    pltpu.make_async_copy(q_ref.at[0, 0, :, first_columns(grp)], first_dst, first_recv).start()
    lax.fori_loop(1, groups, send_first, 0)

    def columns_of(c, g, j):
        return pl.ds(pl.multiple_of((g * heads + first_head(c) + j) * dh, dh), dh)

    def send_head(j, carry):
        for which in ((0, 1), (2,)):
            @pl.when(j < own_count)
            def _():
                for a in which:
                    buf = arrays[a][1]
                    pltpu.make_async_copy(
                        tokens_of(a, columns_of(ctx, grp, j)), buf.at[j, :, my_tokens, :], tok_recv.at[a, j]
                    ).start()

            def send_to(i, inner):
                peer = (me + i) % peers
                c, g = peer // groups, peer % groups

                @pl.when(j < first_head(c + 1) - first_head(c))
                def _():
                    for a in which:
                        buf = arrays[a][1]
                        pltpu.make_async_remote_copy(
                            tokens_of(a, columns_of(c, g, j)), buf.at[j, :, my_tokens, :],
                            tok_send.at[a], tok_recv.at[a, j],
                            device_id=(c, g, core), device_id_type=MESH,
                        ).start()

                return inner

            lax.fori_loop(1, peers, send_to, 0)
        return carry

    lax.fori_loop(0, most, send_head, 0)

    def wait_for(ref, sem):
        pltpu.make_async_copy(ref, ref, sem).wait()

    def answer(queries, weights, gain):
        gate = dot(queries, weights[0])
        up = dot(queries, weights[1])
        hidden = (gate * jax.nn.sigmoid(gate) * up).astype(BF16)
        mapped = dot(hidden, weights[2], 1, 1)
        mean_sq = jnp.mean(mapped * mapped, axis=1, keepdims=True)
        return (mapped * lax.rsqrt(mean_sq + 1e-06) * gain).astype(BF16)

    wait_for(w_buf, w_recv)
    wait_for(first_buf, first_recv)

    def answer_first(h, carry):
        at = pl.ds(pl.multiple_of(h * dh, dh), dh)
        first_out[:, at] = answer(first_buf[:, at], [w_buf[m, h] for m in range(3)], gain_ref[h])
        return carry

    lax.fori_loop(0, heads, answer_first, 0)
    first_copy = pltpu.make_async_copy(first_out, out_ref.at[0, 0], first_send.at[0])
    first_copy.start()
    wait_for(r_buf, r_recv)

    def send_final(head, side, src):
        return pltpu.make_async_remote_copy(
            src, fin_ref.at[:, head], fin_send.at[head, side], fin_recv.at[head],
            device_id=(ctx + (1 if side else -1), grp, core), device_id_type=MESH,
        )

    def relay(step):
        for far in range(1, contexts - 1):
            slot = step - far
            for side in (0, 1):
                owner = ctx - far if side else ctx + far
                exists = (owner >= 0) & (owner < contexts)
                passes = (ctx < contexts - 1) if side else (ctx > 0)
                count = first_head(owner + 1) - first_head(owner)

                @pl.when(exists & passes & (slot >= 0) & (slot < count))
                def _():
                    head = first_head(owner) + slot
                    wait_for(fin_ref.at[:, head], fin_recv.at[head])
                    send_final(head, side, fin_ref.at[:, head]).start()

    chunk = min(tokens, 512)
    chunks = tokens // chunk

    def work(j, carry):
        head = own_first + j
        lane = grp * heads + head
        init_sq = []
        for m in range(3):
            start = w_buf[m, head].astype(F32)
            w_now[m] = start
            init_sq.append(jnp.sqrt(jnp.sum(start * start, axis=0, keepdims=True)))
        wait_for(k_buf.at[j], tok_recv.at[0, j])
        wait_for(v_buf.at[j], tok_recv.at[1, j])

        def block(b, norms):
            for m in range(3):
                w_bf[b, m] = w_now[m].astype(BF16)
                g_acc[m] = jnp.zeros((dh, hf), F32)

            def part(i, total):
                at = pl.ds(pl.multiple_of(i * chunk, chunk), chunk)
                keys, vals = k_buf[j, b, at, :], v_buf[j, b, at, :]
                rate_all = r_buf[b, at, :].astype(F32)
                lanes = lax.broadcasted_iota(jnp.int32, rate_all.shape, 1)
                rate = jnp.sum(jnp.where(lanes == lane, rate_all, 0.0), axis=1, keepdims=True)
                gate = dot(keys, w_bf[b, 0])
                up = dot(keys, w_bf[b, 1])
                back = dot(vals, w_bf[b, 2]) * rate
                sigma = jax.nn.sigmoid(gate)
                act = gate * sigma
                hidden = (act * up).astype(BF16)
                d_up = (back * act).astype(BF16)
                d_gate = (back * up * (sigma * (1.0 + gate * (1.0 - sigma)))).astype(BF16)
                rated = (vals.astype(F32) * rate).astype(BF16)
                g_acc[0] += dot(keys, d_gate, 0, 0)
                g_acc[1] += dot(keys, d_up, 0, 0)
                g_acc[2] += dot(rated, hidden, 0, 0)
                return total + jnp.sum(rate, axis=0, keepdims=True)

            eta = lax.fori_loop(0, chunks, part, jnp.zeros((1, 1), F32)) / tokens
            ortho = []
            for m in range(3):
                grad = g_acc[m]
                frob = jnp.sqrt(jnp.sum(jnp.sum(grad * grad, axis=0, keepdims=True), axis=1, keepdims=True)) + 1e-07
                ortho.append(grad / frob)
            ortho = lax.fori_loop(0, NS_STEPS, lambda s, xs: tuple(schulz_step(x) for x in xs), tuple(ortho))
            for m in range(3):
                moved = w_now[m] + eta * ortho[m]
                scale = norms[m] * lax.rsqrt(jnp.sum(moved * moved, axis=0, keepdims=True) + 1e-06)
                w_now[m] = moved * scale
            return norms

        lax.fori_loop(0, blocks, block, tuple(init_sq))

        for m in range(3):
            f_stage[j, m] = w_now[m].astype(BF16)
        pltpu.make_async_copy(f_stage.at[j], fin_ref.at[:, head], fin_recv.at[head]).start()
        for side in (0, 1):
            @pl.when((ctx < contexts - 1) if side else (ctx > 0))
            def _():
                send_final(head, side, f_stage.at[j]).start()

        relay(j)
        wait_for(q_buf.at[j], tok_recv.at[2, j])
        gain = gain_ref[head]

        def answer_later(b, inner):
            def part(i, innermost):
                at = pl.ds(pl.multiple_of(i * chunk, chunk), chunk)
                o_stage[j, b, at, :] = answer(q_buf[j, b, at, :], [w_bf[b + 1, m] for m in range(3)], gain)
                return innermost

            lax.fori_loop(0, chunks, part, 0)
            return inner

        lax.fori_loop(0, later, answer_later, 0)

        out_dst = out_ref.at[0, pl.ds(1, later), :, pl.ds(pl.multiple_of(head * dh, dh), dh)]

        def of_context(c):
            return o_stage.at[j, :, pl.ds(pl.multiple_of(c * local_tokens, local_tokens), local_tokens), :]

        pltpu.make_async_copy(of_context(ctx), out_dst, out_recv).start()

        def send_out(i, inner):
            c = (ctx + i) % contexts
            pltpu.make_async_remote_copy(
                of_context(c), out_dst, out_send.at[j, i], out_recv,
                device_id=(c, grp, core), device_id_type=MESH,
            ).start()
            return inner

        lax.fori_loop(1, contexts, send_out, 0)
        return carry

    lax.fori_loop(0, own_count, work, 0)

    def relay_rest(step, carry):
        relay(step)
        return carry

    lax.fori_loop(own_count, most + contexts, relay_rest, 0)

    w_remote.wait_send()
    wait_for(r_buf.at[:, 0:tokens - rows, :], r_send)
    for count in sorted({heads // contexts, most}):
        @pl.when(own_count == count)
        def _():
            for a in range(3):
                wait_for(tokens_of(a, pl.ds(0, (groups * heads - count) * dh)), tok_send.at[a])

    first_copy.wait()

    def first_sent(i, carry):
        wait_for(first_dst, first_send.at[i])
        return carry

    lax.fori_loop(1, groups, first_sent, 0)

    def outs_sent(j, carry):
        def one(i, inner):
            wait_for(o_stage.at[j, :, 0:local_tokens, :], out_send.at[j, i])
            return inner

        return lax.fori_loop(1, contexts, one, carry)

    lax.fori_loop(0, own_count, outs_sent, 0)

    def final_done(head, carry):
        from_left = head < own_first
        from_right = head >= own_first + own_count
        to_right, to_left = ctx < contexts - 1, ctx > 0
        went = (to_left & ~from_left, to_right & ~from_right)
        passed = (from_left & to_right) | (from_right & to_left)
        for side in (0, 1):
            @pl.when(went[side])
            def _():
                send_final(head, side, fin_ref.at[:, head]).wait_send()

        @pl.when(~passed)
        def _():
            wait_for(fin_ref.at[:, head], fin_recv.at[head])

        return carry

    lax.fori_loop(0, heads, final_done, 0)
    wait_for(out_ref.at[0, pl.ds(1, later)], out_recv)


def body(contexts, groups, query_tok, key_tok, value_tok, token_rates, fast_init, out_gain):
    _, blocks, rows, _ = query_tok.shape
    _, heads, half, hf = fast_init.shape
    dh = 2 * half
    peers = contexts * groups
    tokens = peers * rows
    most = -(-heads // contexts)
    rates = jnp.pad(token_rates, ((0, 0), (0, 0), (0, 0), (0, 128 - token_rates.shape[3])))
    gain = out_gain.astype(F32).reshape(heads, 1, dh)
    dims = (contexts, groups, heads, blocks, rows, dh, hf)
    anywhere = pl.BlockSpec(memory_space=pl.ANY)
    tok = pltpu.VMEM((most, blocks, tokens, dh), BF16)
    later_tok = pltpu.VMEM((most, blocks - 1, tokens, dh), BF16)
    first_tok = pltpu.VMEM((groups * rows, heads * dh), BF16)
    dma = pltpu.SemaphoreType.DMA
    head_out, final = pl.pallas_call(
        functools.partial(kernel, dims),
        out_shape=(
            jax.ShapeDtypeStruct((1, blocks, groups * rows, heads * dh), BF16),
            jax.ShapeDtypeStruct((3, heads, dh, hf), BF16),
        ),
        in_specs=[anywhere] * 5 + [pl.BlockSpec(memory_space=pltpu.VMEM)],
        out_specs=(anywhere, anywhere),
        scratch_shapes=[
            later_tok, tok, tok,
            pltpu.VMEM((blocks, tokens, 128), BF16),
            pltpu.VMEM((3, heads, dh, hf), BF16),
            first_tok, first_tok,
            later_tok,
            pltpu.VMEM((most, 3, dh, hf), BF16),
            pltpu.VMEM((3, dh, hf), F32),
            pltpu.VMEM((blocks, 3, dh, hf), BF16),
            pltpu.VMEM((3, dh, hf), F32),
            dma((3,)), dma((3, most)), dma((groups,)), dma, dma, dma, dma, dma,
            dma((most, contexts)), dma, dma((heads, 2)), dma((heads,)),
        ],
        compiler_params=pltpu.CompilerParams(
            collective_id=0, has_side_effects=True, vmem_limit_bytes=48 * 1024 * 1024
        ),
    )(query_tok, key_tok, value_tok, rates, fast_init, gain)
    return head_out, final.astype(F32)[None]


def solution(mesh):
    return jax.shard_map(
        functools.partial(body, mesh.shape["context"], mesh.shape["head"]),
        mesh=mesh,
        in_specs=(
            P("dp", None, ("context", "head"), None),
            P("dp", None, ("context", "head"), None),
            P("dp", None, ("context", "head"), None),
            P("dp", None, ("context", "head"), None),
            P(None, "head", "dp", None),
            P("head"),
        ),
        out_specs=(P("dp", None, "context", "head"), P("dp", None, "head", None, None)),
        check_vma=False,
    )
```

```python
import functools

import jax
import jax.numpy as jnp
from jax import lax
from jax.experimental import pallas as pl
from jax.experimental.pallas import tpu as pltpu
from jax.sharding import PartitionSpec as P

NS_STEPS = 5
COEFFS = (3.4445, -4.775, 2.0315)
MESH = pl.DeviceIdType.MESH
F32 = jnp.float32
BF16 = jnp.bfloat16


def dot(a, b, ca=1, cb=0):
    return lax.dot_general(a, b, (((ca,), (cb,)), ((), ())), preferred_element_type=F32)


def split(x):
    high = x.astype(BF16)
    return high, (x - high.astype(F32)).astype(BF16)


def schulz_step(ortho):
    xh, xl = split(ortho)
    both = dot(xh, jnp.concatenate([xh, xl], axis=0), 1, 1)
    half = both.shape[1] // 2
    cross = both[:, half:]
    gram = both[:, :half] + cross + cross.T
    gh, gl = split(gram)
    both = dot(gh, jnp.concatenate([gh, gl], axis=1))
    cross = both[:, half:]
    poly = COEFFS[1] * gram + COEFFS[2] * (both[:, :half] + cross + cross.T)
    ph, pl_ = split(poly)
    moved = dot(jnp.concatenate([ph, pl_], axis=1), jnp.concatenate([xh, xh], axis=0)) + dot(ph, xl)
    return COEFFS[0] * ortho + moved


def kernel(
    dims,
    q_ref, k_ref, v_ref, r_ref, w_ref, gain_ref,
    out_ref, fin_ref,
    q_buf, k_buf, v_buf, r_buf, w_buf, first_buf, first_out, o_stage, f_stage,
    w_now, w_bf, g_acc,
    tok_send, tok_recv, first_send, first_recv, r_send, r_recv, w_send, w_recv,
    out_send, out_recv, fin_send, fin_recv,
):
    contexts, groups, heads, blocks, rows, dh, hf = dims
    peers = contexts * groups
    tokens = peers * rows
    local_tokens = groups * rows
    ctx, grp, core = lax.axis_index("context"), lax.axis_index("head"), lax.axis_index("dp")
    me = ctx * groups + grp

    def first_head(c):
        return (c * heads) // contexts

    own_first = first_head(ctx)
    own_count = first_head(ctx + 1) - own_first
    most = -(-heads // contexts)

    barrier = pltpu.get_barrier_semaphore()

    def greet(i, carry):
        peer = (me + i) % peers
        pl.semaphore_signal(barrier, inc=1, device_id=(peer // groups, peer % groups, core), device_id_type=MESH)
        return carry

    lax.fori_loop(1, peers, greet, 0)
    pl.semaphore_signal(barrier, inc=1, device_id=(ctx, grp, 1 - core), device_id_type=MESH)
    pl.semaphore_wait(barrier, peers)

    my_rows = pl.ds(pl.multiple_of(core * (dh // 2), dh // 2), dh // 2)
    w_src = w_ref
    w_dst = w_buf.at[:, :, my_rows, :]
    w_remote = pltpu.make_async_remote_copy(
        w_src, w_dst, w_send, w_recv, device_id=(ctx, grp, 1 - core), device_id_type=MESH
    )
    w_remote.start()
    pltpu.make_async_copy(w_src, w_dst, w_recv).start()

    my_tokens = pl.ds(pl.multiple_of(me * rows, rows), rows)
    r_dst = r_buf.at[my_tokens, :]
    pltpu.make_async_copy(r_ref, r_dst, r_recv).start()

    def send_rates(i, carry):
        peer = (me + i) % peers
        pltpu.make_async_remote_copy(
            r_ref, r_dst, r_send, r_recv,
            device_id=(peer // groups, peer % groups, core), device_id_type=MESH,
        ).start()
        return carry

    lax.fori_loop(1, peers, send_rates, 0)

    later = blocks - 1
    arrays = ((k_ref, k_buf, blocks), (v_ref, v_buf, blocks), (q_ref, q_buf, later))

    def tokens_of(a, where):
        src, _, count = arrays[a]
        return src.at[0, pl.ds(blocks - count, count), :, where]

    def first_columns(g):
        return pl.ds(pl.multiple_of(g * heads * dh, heads * dh), heads * dh)

    first_dst = first_buf.at[pl.ds(pl.multiple_of(grp * rows, rows), rows), :]

    def send_first(i, carry):
        g = (grp + i) % groups
        pltpu.make_async_remote_copy(
            q_ref.at[0, 0, :, first_columns(g)], first_dst, first_send.at[i], first_recv,
            device_id=(ctx, g, core), device_id_type=MESH,
        ).start()
        return carry

    def columns_of(c, g, j):
        return pl.ds(pl.multiple_of((g * heads + first_head(c) + j) * dh, dh), dh)

    def send_head(j, carry):
        for which in ((0, 1), (2,)):
            @pl.when(j < own_count)
            def _():
                for a in which:
                    buf = arrays[a][1]
                    pltpu.make_async_copy(
                        tokens_of(a, columns_of(ctx, grp, j)), buf.at[j, :, my_tokens, :], tok_recv.at[a, j]
                    ).start()

            def send_to(i, inner):
                peer = (me + i) % peers
                c, g = peer // groups, peer % groups

                @pl.when(j < first_head(c + 1) - first_head(c))
                def _():
                    for a in which:
                        buf = arrays[a][1]
                        pltpu.make_async_remote_copy(
                            tokens_of(a, columns_of(c, g, j)), buf.at[j, :, my_tokens, :],
                            tok_send.at[a], tok_recv.at[a, j],
                            device_id=(c, g, core), device_id_type=MESH,
                        ).start()

                return inner

            lax.fori_loop(1, peers, send_to, 0)
        return carry

    lax.fori_loop(0, 1, send_head, 0)
    pltpu.make_async_copy(q_ref.at[0, 0, :, first_columns(grp)], first_dst, first_recv).start()
    lax.fori_loop(1, groups, send_first, 0)

    def wait_for(ref, sem):
        pltpu.make_async_copy(ref, ref, sem).wait()

    def answer(queries, weights, gain):
        gate = dot(queries, weights[0])
        up = dot(queries, weights[1])
        hidden = (gate * jax.nn.sigmoid(gate) * up).astype(BF16)
        mapped = dot(hidden, weights[2], 1, 1)
        mean_sq = jnp.mean(mapped * mapped, axis=1, keepdims=True)
        return (mapped * lax.rsqrt(mean_sq + 1e-06) * gain).astype(BF16)

    wait_for(w_buf, w_recv)
    wait_for(first_buf, first_recv)

    def answer_first(h, carry):
        at = pl.ds(pl.multiple_of(h * dh, dh), dh)
        first_out[:, at] = answer(first_buf[:, at], [w_buf[m, h] for m in range(3)], gain_ref[h])
        return carry

    lax.fori_loop(0, heads, answer_first, 0)
    lax.fori_loop(1, most, send_head, 0)
    first_copy = pltpu.make_async_copy(first_out, out_ref.at[0, 0], first_send.at[0])
    first_copy.start()
    wait_for(r_buf, r_recv)

    def send_final(head, side, src):
        return pltpu.make_async_remote_copy(
            src, fin_ref.at[:, head], fin_send.at[head, side], fin_recv.at[head],
            device_id=(ctx + (1 if side else -1), grp, core), device_id_type=MESH,
        )

    def relay(step, low, high):
        for far in range(low, high):
            slot = step - max(far - 1, 1)
            for side in (0, 1):
                owner = ctx - far if side else ctx + far
                exists = (owner >= 0) & (owner < contexts)
                passes = (ctx < contexts - 1) if side else (ctx > 0)
                count = first_head(owner + 1) - first_head(owner)

                @pl.when(exists & passes & (slot >= 0) & (slot < count))
                def _():
                    head = first_head(owner) + slot
                    wait_for(fin_ref.at[:, head], fin_recv.at[head])
                    send_final(head, side, fin_ref.at[:, head]).start()

    chunk = min(tokens, 512)
    chunks = tokens // chunk

    def work(j, carry):
        head = own_first + j
        lane = grp * heads + head
        init_sq = []
        for m in range(3):
            start = w_buf[m, head].astype(F32)
            w_now[m] = start
            init_sq.append(jnp.sqrt(jnp.sum(start * start, axis=0, keepdims=True)))
        wait_for(k_buf.at[j], tok_recv.at[0, j])
        wait_for(v_buf.at[j], tok_recv.at[1, j])

        def block(b, norms):
            @pl.when(b == blocks - 1)
            def _():
                relay(j, 1, min(2, contexts - 1))

            for m in range(3):
                w_bf[b, m] = w_now[m].astype(BF16)
                g_acc[m] = jnp.zeros((dh, hf), F32)

            def part(i, total):
                at = pl.ds(pl.multiple_of(i * chunk, chunk), chunk)
                keys, vals = k_buf[j, b, at, :], v_buf[j, b, at, :]
                rate_all = r_buf[at, :].astype(F32)
                lanes = lax.broadcasted_iota(jnp.int32, rate_all.shape, 1)
                rate = jnp.sum(jnp.where(lanes == lane + b * (groups * heads), rate_all, 0.0), axis=1, keepdims=True)
                gate = dot(keys, w_bf[b, 0])
                up = dot(keys, w_bf[b, 1])
                back = dot(vals, w_bf[b, 2]) * rate
                sigma = jax.nn.sigmoid(gate)
                act = gate * sigma
                hidden = (act * up).astype(BF16)
                d_up = (back * act).astype(BF16)
                d_gate = (back * up * (sigma * (1.0 + gate * (1.0 - sigma)))).astype(BF16)
                rated = (vals.astype(F32) * rate).astype(BF16)
                g_acc[0] += dot(keys, d_gate, 0, 0)
                g_acc[1] += dot(keys, d_up, 0, 0)
                g_acc[2] += dot(rated, hidden, 0, 0)
                return total + jnp.sum(rate, axis=0, keepdims=True)

            eta = lax.fori_loop(0, chunks, part, jnp.zeros((1, 1), F32)) / tokens
            ortho = []
            for m in range(3):
                grad = g_acc[m]
                frob = jnp.sqrt(jnp.sum(jnp.sum(grad * grad, axis=0, keepdims=True), axis=1, keepdims=True)) + 1e-07
                ortho.append(grad / frob)
            ortho = lax.fori_loop(0, NS_STEPS, lambda s, xs: tuple(schulz_step(x) for x in xs), tuple(ortho))
            for m in range(3):
                moved = w_now[m] + eta * ortho[m]
                scale = norms[m] * lax.rsqrt(jnp.sum(moved * moved, axis=0, keepdims=True) + 1e-06)
                w_now[m] = moved * scale
            return norms

        lax.fori_loop(0, blocks, block, tuple(init_sq))

        for m in range(3):
            f_stage[j, m] = w_now[m].astype(BF16)
        pltpu.make_async_copy(f_stage.at[j], fin_ref.at[:, head], fin_recv.at[head]).start()
        for side in (0, 1):
            @pl.when((ctx < contexts - 1) if side else (ctx > 0))
            def _():
                send_final(head, side, f_stage.at[j]).start()

        relay(j, 2, contexts - 1)
        wait_for(q_buf.at[j], tok_recv.at[2, j])
        gain = gain_ref[head]

        def answer_later(b, inner):
            def part(i, innermost):
                at = pl.ds(pl.multiple_of(i * chunk, chunk), chunk)
                o_stage[j, b, at, :] = answer(q_buf[j, b, at, :], [w_bf[b + 1, m] for m in range(3)], gain)
                return innermost

            lax.fori_loop(0, chunks, part, 0)
            return inner

        lax.fori_loop(0, later, answer_later, 0)

        out_dst = out_ref.at[0, pl.ds(1, later), :, pl.ds(pl.multiple_of(head * dh, dh), dh)]

        def of_context(c):
            return o_stage.at[j, :, pl.ds(pl.multiple_of(c * local_tokens, local_tokens), local_tokens), :]

        pltpu.make_async_copy(of_context(ctx), out_dst, out_recv).start()

        def send_out(i, inner):
            c = (ctx + i) % contexts
            pltpu.make_async_remote_copy(
                of_context(c), out_dst, out_send.at[j, i], out_recv,
                device_id=(c, grp, core), device_id_type=MESH,
            ).start()
            return inner

        lax.fori_loop(1, contexts, send_out, 0)
        return carry

    lax.fori_loop(0, own_count, work, 0)

    def relay_rest(step, carry):
        relay(step, 1, contexts - 1)
        return carry

    lax.fori_loop(own_count, most + contexts, relay_rest, 0)

    w_remote.wait_send()
    wait_for(r_buf.at[0:tokens - rows, :], r_send)
    for count in sorted({heads // contexts, most}):
        @pl.when(own_count == count)
        def _():
            for a in range(3):
                wait_for(tokens_of(a, pl.ds(0, (groups * heads - count) * dh)), tok_send.at[a])

    first_copy.wait()

    def first_sent(i, carry):
        wait_for(first_dst, first_send.at[i])
        return carry

    lax.fori_loop(1, groups, first_sent, 0)

    def outs_sent(j, carry):
        def one(i, inner):
            wait_for(o_stage.at[j, :, 0:local_tokens, :], out_send.at[j, i])
            return inner

        return lax.fori_loop(1, contexts, one, carry)

    lax.fori_loop(0, own_count, outs_sent, 0)

    def final_done(head, carry):
        from_left = head < own_first
        from_right = head >= own_first + own_count
        to_right, to_left = ctx < contexts - 1, ctx > 0
        went = (to_left & ~from_left, to_right & ~from_right)
        passed = (from_left & to_right) | (from_right & to_left)
        for side in (0, 1):
            @pl.when(went[side])
            def _():
                send_final(head, side, fin_ref.at[:, head]).wait_send()

        @pl.when(~passed)
        def _():
            wait_for(fin_ref.at[:, head], fin_recv.at[head])

        return carry

    lax.fori_loop(0, heads, final_done, 0)
    wait_for(out_ref.at[0, pl.ds(1, later)], out_recv)


def body(contexts, groups, query_tok, key_tok, value_tok, token_rates, fast_init, out_gain):
    _, blocks, rows, _ = query_tok.shape
    _, heads, half, hf = fast_init.shape
    dh = 2 * half
    peers = contexts * groups
    tokens = peers * rows
    most = -(-heads // contexts)
    rates = token_rates[0].transpose(1, 0, 2).reshape(rows, -1)
    rates = jnp.pad(rates, ((0, 0), (0, -rates.shape[1] % 128)))
    gain = out_gain.astype(F32).reshape(heads, 1, dh)
    dims = (contexts, groups, heads, blocks, rows, dh, hf)
    anywhere = pl.BlockSpec(memory_space=pl.ANY)
    tok = pltpu.VMEM((most, blocks, tokens, dh), BF16)
    later_tok = pltpu.VMEM((most, blocks - 1, tokens, dh), BF16)
    first_tok = pltpu.VMEM((groups * rows, heads * dh), BF16)
    dma = pltpu.SemaphoreType.DMA
    head_out, final = pl.pallas_call(
        functools.partial(kernel, dims),
        out_shape=(
            jax.ShapeDtypeStruct((1, blocks, groups * rows, heads * dh), BF16),
            jax.ShapeDtypeStruct((3, heads, dh, hf), BF16),
        ),
        in_specs=[anywhere] * 5 + [pl.BlockSpec(memory_space=pltpu.VMEM)],
        out_specs=(anywhere, anywhere),
        scratch_shapes=[
            later_tok, tok, tok,
            pltpu.VMEM((tokens, rates.shape[1]), BF16),
            pltpu.VMEM((3, heads, dh, hf), BF16),
            first_tok, first_tok,
            later_tok,
            pltpu.VMEM((most, 3, dh, hf), BF16),
            pltpu.VMEM((3, dh, hf), F32),
            pltpu.VMEM((blocks, 3, dh, hf), BF16),
            pltpu.VMEM((3, dh, hf), F32),
            dma((3,)), dma((3, most)), dma((groups,)), dma, dma, dma, dma, dma,
            dma((most, contexts)), dma, dma((heads, 2)), dma((heads,)),
        ],
        compiler_params=pltpu.CompilerParams(
            collective_id=0, has_side_effects=True, vmem_limit_bytes=48 * 1024 * 1024
        ),
    )(query_tok, key_tok, value_tok, rates, fast_init, gain)
    return head_out, final.astype(F32)[None]


def solution(mesh):
    return jax.shard_map(
        functools.partial(body, mesh.shape["context"], mesh.shape["head"]),
        mesh=mesh,
        in_specs=(
            P("dp", None, ("context", "head"), None),
            P("dp", None, ("context", "head"), None),
            P("dp", None, ("context", "head"), None),
            P("dp", None, ("context", "head"), None),
            P(None, "head", "dp", None),
            P("head"),
        ),
        out_specs=(P("dp", None, "context", "head"), P("dp", None, "head", None, None)),
        check_vma=False,
    )
```

```python
import functools

import jax
import jax.numpy as jnp
from jax import lax
from jax.experimental import pallas as pl
from jax.experimental.pallas import tpu as pltpu
from jax.sharding import PartitionSpec as P

NS_STEPS = 5
COEFFS = (3.4445, -4.775, 2.0315)
MESH = pl.DeviceIdType.MESH
F32 = jnp.float32
BF16 = jnp.bfloat16


def dot(a, b, ca=1, cb=0):
    return lax.dot_general(a, b, (((ca,), (cb,)), ((), ())), preferred_element_type=F32)


def split(x):
    high = x.astype(BF16)
    return high, (x - high.astype(F32)).astype(BF16)


def schulz_step(ortho):
    xh, xl = split(ortho)
    both = dot(xh, jnp.concatenate([xh, xl], axis=0), 1, 1)
    half = both.shape[1] // 2
    cross = both[:, half:]
    gram = both[:, :half] + cross + cross.T
    gh, gl = split(gram)
    both = dot(gh, jnp.concatenate([gh, gl], axis=1))
    cross = both[:, half:]
    poly = COEFFS[1] * gram + COEFFS[2] * (both[:, :half] + cross + cross.T)
    ph, pl_ = split(poly)
    moved = dot(jnp.concatenate([ph, pl_], axis=1), jnp.concatenate([xh, xh], axis=0)) + dot(ph, xl)
    return COEFFS[0] * ortho + moved


def kernel(
    dims,
    q_ref, k_ref, v_ref, r_ref, w_ref, gain_ref,
    out_ref, fin_ref,
    q_buf, k_buf, v_buf, r_buf, w_buf, first_buf, first_out, o_stage, f_stage,
    w_now, w_bf, g_acc,
    tok_send, tok_recv, first_send, first_recv, r_send, r_recv, w_send, w_recv,
    out_send, out_recv, fin_send, fin_recv,
):
    contexts, groups, heads, blocks, rows, dh, hf = dims
    peers = contexts * groups
    tokens = peers * rows
    local_tokens = groups * rows
    ctx, grp, core = lax.axis_index("context"), lax.axis_index("head"), lax.axis_index("dp")
    me = ctx * groups + grp

    def first_head(c):
        return (c * heads) // contexts

    own_first = first_head(ctx)
    own_count = first_head(ctx + 1) - own_first
    most = -(-heads // contexts)

    barrier = pltpu.get_barrier_semaphore()

    def greet(i, carry):
        peer = (me + i) % peers
        pl.semaphore_signal(barrier, inc=1, device_id=(peer // groups, peer % groups, core), device_id_type=MESH)
        return carry

    lax.fori_loop(1, peers, greet, 0)
    pl.semaphore_signal(barrier, inc=1, device_id=(ctx, grp, 1 - core), device_id_type=MESH)
    pl.semaphore_wait(barrier, peers)

    my_rows = pl.ds(pl.multiple_of(core * (dh // 2), dh // 2), dh // 2)
    w_src = w_ref
    w_dst = w_buf.at[:, :, my_rows, :]
    w_remote = pltpu.make_async_remote_copy(
        w_src, w_dst, w_send, w_recv, device_id=(ctx, grp, 1 - core), device_id_type=MESH
    )
    w_remote.start()
    pltpu.make_async_copy(w_src, w_dst, w_recv).start()

    my_tokens = pl.ds(pl.multiple_of(me * rows, rows), rows)
    r_dst = r_buf.at[my_tokens, :]
    pltpu.make_async_copy(r_ref, r_dst, r_recv).start()

    def send_rates(i, carry):
        peer = (me + i) % peers
        pltpu.make_async_remote_copy(
            r_ref, r_dst, r_send, r_recv,
            device_id=(peer // groups, peer % groups, core), device_id_type=MESH,
        ).start()
        return carry

    lax.fori_loop(1, peers, send_rates, 0)

    later = blocks - 1
    arrays = ((k_ref, k_buf, blocks), (v_ref, v_buf, blocks), (q_ref, q_buf, later))

    def tokens_of(a, where):
        src, _, count = arrays[a]
        return src.at[0, pl.ds(blocks - count, count), :, where]

    def first_columns(g):
        return pl.ds(pl.multiple_of(g * heads * dh, heads * dh), heads * dh)

    first_dst = first_buf.at[pl.ds(pl.multiple_of(grp * rows, rows), rows), :]

    def send_first(i, carry):
        g = (grp + i) % groups
        pltpu.make_async_remote_copy(
            q_ref.at[0, 0, :, first_columns(g)], first_dst, first_send.at[i], first_recv,
            device_id=(ctx, g, core), device_id_type=MESH,
        ).start()
        return carry

    def columns_of(c, g, j):
        return pl.ds(pl.multiple_of((g * heads + first_head(c) + j) * dh, dh), dh)

    def send_head(j, carry):
        for which in ((0, 1), (2,)):
            @pl.when(j < own_count)
            def _():
                for a in which:
                    buf = arrays[a][1]
                    pltpu.make_async_copy(
                        tokens_of(a, columns_of(ctx, grp, j)), buf.at[j, :, my_tokens, :], tok_recv.at[a, j]
                    ).start()

            def send_to(i, inner):
                peer = (me + i) % peers
                c, g = peer // groups, peer % groups

                @pl.when(j < first_head(c + 1) - first_head(c))
                def _():
                    for a in which:
                        buf = arrays[a][1]
                        pltpu.make_async_remote_copy(
                            tokens_of(a, columns_of(c, g, j)), buf.at[j, :, my_tokens, :],
                            tok_send.at[a], tok_recv.at[a, j],
                            device_id=(c, g, core), device_id_type=MESH,
                        ).start()

                return inner

            lax.fori_loop(1, peers, send_to, 0)
        return carry

    lax.fori_loop(0, 1, send_head, 0)
    pltpu.make_async_copy(q_ref.at[0, 0, :, first_columns(grp)], first_dst, first_recv).start()
    lax.fori_loop(1, groups, send_first, 0)

    def wait_for(ref, sem):
        pltpu.make_async_copy(ref, ref, sem).wait()

    def answer(queries, weights, gain):
        gate = dot(queries, weights[0])
        up = dot(queries, weights[1])
        hidden = (gate * jax.nn.sigmoid(gate) * up).astype(BF16)
        mapped = dot(hidden, weights[2], 1, 1)
        mean_sq = jnp.mean(mapped * mapped, axis=1, keepdims=True)
        return (mapped * lax.rsqrt(mean_sq + 1e-06) * gain).astype(BF16)

    wait_for(w_buf, w_recv)
    wait_for(first_buf, first_recv)

    def answer_first(h, carry):
        at = pl.ds(pl.multiple_of(h * dh, dh), dh)
        first_out[:, at] = answer(first_buf[:, at], [w_buf[m, h] for m in range(3)], gain_ref[h])
        return carry

    lax.fori_loop(0, heads, answer_first, 0)
    lax.fori_loop(1, most, send_head, 0)
    first_copy = pltpu.make_async_copy(first_out, out_ref.at[0, 0], first_send.at[0])
    first_copy.start()
    wait_for(r_buf, r_recv)

    def send_final(head, side, src):
        return pltpu.make_async_remote_copy(
            src, fin_ref.at[:, head], fin_send.at[head, side], fin_recv.at[head],
            device_id=(ctx + (1 if side else -1), grp, core), device_id_type=MESH,
        )

    def relay(step, low, high):
        for far in range(low, high):
            slot = step - max(far - 1, 1)
            for side in (0, 1):
                owner = ctx - far if side else ctx + far
                exists = (owner >= 0) & (owner < contexts)
                passes = (ctx < contexts - 1) if side else (ctx > 0)
                count = first_head(owner + 1) - first_head(owner)

                @pl.when(exists & passes & (slot >= 0) & (slot < count))
                def _():
                    head = first_head(owner) + slot
                    wait_for(fin_ref.at[:, head], fin_recv.at[head])
                    send_final(head, side, fin_ref.at[:, head]).start()

    chunk = min(tokens, 512)
    chunks = tokens // chunk

    def work(j, carry):
        head = own_first + j
        lane = grp * heads + head
        init_sq = []
        for m in range(3):
            start = w_buf[m, head].astype(F32)
            w_now[m] = start
            init_sq.append(jnp.sqrt(jnp.sum(start * start, axis=0, keepdims=True)))
        wait_for(k_buf.at[j], tok_recv.at[0, j])
        wait_for(v_buf.at[j], tok_recv.at[1, j])

        def block(b, norms):
            @pl.when(b == blocks - 1)
            def _():
                relay(j, 1, min(2, contexts - 1))

            for m in range(3):
                w_bf[b, m] = w_now[m].astype(BF16)
                g_acc[m] = jnp.zeros((dh, hf), F32)

            def part(i, total):
                at = pl.ds(pl.multiple_of(i * chunk, chunk), chunk)
                keys, vals = k_buf[j, b, at, :], v_buf[j, b, at, :]
                rate_all = r_buf[at, :].astype(F32)
                lanes = lax.broadcasted_iota(jnp.int32, rate_all.shape, 1)
                rate = jnp.sum(jnp.where(lanes == lane + b * (groups * heads), rate_all, 0.0), axis=1, keepdims=True)
                gate = dot(keys, w_bf[b, 0])
                up = dot(keys, w_bf[b, 1])
                back = dot(vals, w_bf[b, 2]) * rate
                sigma = jax.nn.sigmoid(gate)
                act = gate * sigma
                hidden = (act * up).astype(BF16)
                d_up = (back * act).astype(BF16)
                d_gate = (back * up * (sigma * (1.0 + gate * (1.0 - sigma)))).astype(BF16)
                rated = (vals.astype(F32) * rate).astype(BF16)
                g_acc[0] += dot(keys, d_gate, 0, 0)
                g_acc[1] += dot(keys, d_up, 0, 0)
                g_acc[2] += dot(rated, hidden, 0, 0)
                return total + jnp.sum(rate, axis=0, keepdims=True)

            eta = lax.fori_loop(0, chunks, part, jnp.zeros((1, 1), F32)) / tokens
            ortho = []
            for m in range(3):
                grad = g_acc[m]
                frob = jnp.sqrt(jnp.sum(jnp.sum(grad * grad, axis=0, keepdims=True), axis=1, keepdims=True)) + 1e-07
                ortho.append(grad / frob)
            ortho = lax.fori_loop(0, NS_STEPS, lambda s, xs: tuple(schulz_step(x) for x in xs), tuple(ortho), unroll=True)
            for m in range(3):
                moved = w_now[m] + eta * ortho[m]
                scale = norms[m] * lax.rsqrt(jnp.sum(moved * moved, axis=0, keepdims=True) + 1e-06)
                w_now[m] = moved * scale
            return norms

        lax.fori_loop(0, blocks, block, tuple(init_sq))

        for m in range(3):
            f_stage[j, m] = w_now[m].astype(BF16)
        pltpu.make_async_copy(f_stage.at[j], fin_ref.at[:, head], fin_recv.at[head]).start()
        for side in (0, 1):
            @pl.when((ctx < contexts - 1) if side else (ctx > 0))
            def _():
                send_final(head, side, f_stage.at[j]).start()

        relay(j, 2, contexts - 1)
        wait_for(q_buf.at[j], tok_recv.at[2, j])
        gain = gain_ref[head]

        def answer_later(b, inner):
            def part(i, innermost):
                at = pl.ds(pl.multiple_of(i * chunk, chunk), chunk)
                o_stage[j, b, at, :] = answer(q_buf[j, b, at, :], [w_bf[b + 1, m] for m in range(3)], gain)
                return innermost

            lax.fori_loop(0, chunks, part, 0)
            return inner

        lax.fori_loop(0, later, answer_later, 0)

        out_dst = out_ref.at[0, pl.ds(1, later), :, pl.ds(pl.multiple_of(head * dh, dh), dh)]

        def of_context(c):
            return o_stage.at[j, :, pl.ds(pl.multiple_of(c * local_tokens, local_tokens), local_tokens), :]

        pltpu.make_async_copy(of_context(ctx), out_dst, out_recv).start()

        def send_out(i, inner):
            c = (ctx + i) % contexts
            pltpu.make_async_remote_copy(
                of_context(c), out_dst, out_send.at[j, i], out_recv,
                device_id=(c, grp, core), device_id_type=MESH,
            ).start()
            return inner

        lax.fori_loop(1, contexts, send_out, 0)
        return carry

    lax.fori_loop(0, own_count, work, 0)

    def relay_rest(step, carry):
        relay(step, 1, contexts - 1)
        return carry

    lax.fori_loop(own_count, most + contexts, relay_rest, 0)

    w_remote.wait_send()
    wait_for(r_buf.at[0:tokens - rows, :], r_send)
    for count in sorted({heads // contexts, most}):
        @pl.when(own_count == count)
        def _():
            for a in range(3):
                wait_for(tokens_of(a, pl.ds(0, (groups * heads - count) * dh)), tok_send.at[a])

    first_copy.wait()

    def first_sent(i, carry):
        wait_for(first_dst, first_send.at[i])
        return carry

    lax.fori_loop(1, groups, first_sent, 0)

    def outs_sent(j, carry):
        def one(i, inner):
            wait_for(o_stage.at[j, :, 0:local_tokens, :], out_send.at[j, i])
            return inner

        return lax.fori_loop(1, contexts, one, carry)

    lax.fori_loop(0, own_count, outs_sent, 0)

    def final_done(head, carry):
        from_left = head < own_first
        from_right = head >= own_first + own_count
        to_right, to_left = ctx < contexts - 1, ctx > 0
        went = (to_left & ~from_left, to_right & ~from_right)
        passed = (from_left & to_right) | (from_right & to_left)
        for side in (0, 1):
            @pl.when(went[side])
            def _():
                send_final(head, side, fin_ref.at[:, head]).wait_send()

        @pl.when(~passed)
        def _():
            wait_for(fin_ref.at[:, head], fin_recv.at[head])

        return carry

    lax.fori_loop(0, heads, final_done, 0)
    wait_for(out_ref.at[0, pl.ds(1, later)], out_recv)


def body(contexts, groups, query_tok, key_tok, value_tok, token_rates, fast_init, out_gain):
    _, blocks, rows, _ = query_tok.shape
    _, heads, half, hf = fast_init.shape
    dh = 2 * half
    peers = contexts * groups
    tokens = peers * rows
    most = -(-heads // contexts)
    rates = token_rates[0].transpose(1, 0, 2).reshape(rows, -1)
    rates = jnp.pad(rates, ((0, 0), (0, -rates.shape[1] % 128)))
    gain = out_gain.astype(F32).reshape(heads, 1, dh)
    dims = (contexts, groups, heads, blocks, rows, dh, hf)
    anywhere = pl.BlockSpec(memory_space=pl.ANY)
    tok = pltpu.VMEM((most, blocks, tokens, dh), BF16)
    later_tok = pltpu.VMEM((most, blocks - 1, tokens, dh), BF16)
    first_tok = pltpu.VMEM((groups * rows, heads * dh), BF16)
    dma = pltpu.SemaphoreType.DMA
    head_out, final = pl.pallas_call(
        functools.partial(kernel, dims),
        out_shape=(
            jax.ShapeDtypeStruct((1, blocks, groups * rows, heads * dh), BF16),
            jax.ShapeDtypeStruct((3, heads, dh, hf), BF16),
        ),
        in_specs=[anywhere] * 5 + [pl.BlockSpec(memory_space=pltpu.VMEM)],
        out_specs=(anywhere, anywhere),
        scratch_shapes=[
            later_tok, tok, tok,
            pltpu.VMEM((tokens, rates.shape[1]), BF16),
            pltpu.VMEM((3, heads, dh, hf), BF16),
            first_tok, first_tok,
            later_tok,
            pltpu.VMEM((most, 3, dh, hf), BF16),
            pltpu.VMEM((3, dh, hf), F32),
            pltpu.VMEM((blocks, 3, dh, hf), BF16),
            pltpu.VMEM((3, dh, hf), F32),
            dma((3,)), dma((3, most)), dma((groups,)), dma, dma, dma, dma, dma,
            dma((most, contexts)), dma, dma((heads, 2)), dma((heads,)),
        ],
        compiler_params=pltpu.CompilerParams(
            collective_id=0, has_side_effects=True, vmem_limit_bytes=48 * 1024 * 1024
        ),
    )(query_tok, key_tok, value_tok, rates, fast_init, gain)
    return head_out, final.astype(F32)[None]


def solution(mesh):
    return jax.shard_map(
        functools.partial(body, mesh.shape["context"], mesh.shape["head"]),
        mesh=mesh,
        in_specs=(
            P("dp", None, ("context", "head"), None),
            P("dp", None, ("context", "head"), None),
            P("dp", None, ("context", "head"), None),
            P("dp", None, ("context", "head"), None),
            P(None, "head", "dp", None),
            P("head"),
        ),
        out_specs=(P("dp", None, "context", "head"), P("dp", None, "head", None, None)),
        check_vma=False,
    )
```
